256 devices in a mesh: dp: 32 (over x_hi, z, core), tensor: 8 (over x_lo, y).
Axes of the slice: x: 4 (x_hi: 2, x_lo: 2; x = x_hi * 2 + x_lo), y: 4, z: 8, core: 2. Of those that a mesh axis runs over, the one named last changes fastest.
Arguments:
- acts: bfloat16 [65536, 8192], P('dp', 'tensor'), may hold values from -6 to 6
- cotangent: bfloat16 [65536, 8192], P(('dp', 'tensor')), may hold values from -6 to 6
- down_weight: bfloat16 [8192, 16], P('tensor'), may hold values from -0.0625 to 0.0625
- project: bfloat16 [8192, 512], P('tensor'), may hold values from -0.0625 to 0.0625
- queries: bfloat16 [4096, 8192], P('dp', 'tensor'), may hold values from -6 to 6
Outputs:
- scores: float32 [4096, 64], P('dp')
The draws below stay inside these ranges and needn't reach their ends.
All inputs are finite; a program needn't handle non-finite values.
Results may differ from the reference program's by a relative error of at most 0.0041.
Values may be sent and summed in bfloat16 or wider, within the bound.
A program may use at most 64 MiB of HBM per device.

```python
import jax
import jax.numpy as jnp
from jax import lax

MODEL_WIDTH = 8192
ADAPTER_RANK = 16
PK = 512
LENGTH = 1024
TRAIN_SEQUENCES = 64
QUERIES = 4096
K = 8192


def shard_levels(key, extent, pieces, smallest, largest):
    gain = 1.0
    for position, blocks in pieces:
        draws = jax.random.uniform(jax.random.fold_in(jax.random.fold_in(key, 6), position), (blocks,), jnp.float32, smallest / len(pieces), largest / len(pieces))
        gain = gain * jnp.repeat(jnp.exp(draws), extent[position] // blocks).reshape((-1,) + (1,) * (len(extent) - 1 - position))
    return gain


def bell_draw(key, dims, deviation, most, shards=(), kind=jnp.bfloat16):
    array = deviation * jax.random.normal(key, dims, jnp.float32)
    if shards:
        array = array * shard_levels(key, dims, shards, -0.22, 0.18)
    return jnp.clip(array, -most, most).astype(kind)


def setup_inputs(seed: int = 0) -> dict:
    arg_keys = jax.random.split(jax.random.key(seed), 6)
    acts = bell_draw(arg_keys[0], (TRAIN_SEQUENCES * LENGTH, MODEL_WIDTH), 1.0, 6.0, ((0, 32), (1, 8)))
    cotangent = bell_draw(arg_keys[1], (TRAIN_SEQUENCES * LENGTH, MODEL_WIDTH), 1.0, 6.0, ((0, 256),))
    down_weight = bell_draw(arg_keys[2], (MODEL_WIDTH, ADAPTER_RANK), MODEL_WIDTH ** -0.5, 0.0625, ((0, 8),))
    project = bell_draw(arg_keys[3], (MODEL_WIDTH, PK), MODEL_WIDTH ** -0.5, 0.0625, ((0, 8),))
    queries = bell_draw(arg_keys[4], (QUERIES, K), 1.0, 6.0, ((0, 32), (1, 8)))
    return {"acts": acts, "cotangent": cotangent, "down_weight": down_weight, "project": project, "queries": queries}


def solve_factor(factor, rhs):
    middle = lax.linalg.triangular_solve(factor, rhs, left_side=True, lower=True, transpose_a=False)
    return lax.linalg.triangular_solve(factor, middle, left_side=True, lower=True, transpose_a=True)

def reference(acts, cotangent, down_weight, project, queries):
    input_rows = jnp.dot(acts.astype(jnp.float32), down_weight.astype(jnp.float32), preferred_element_type=jnp.float32).astype(jnp.bfloat16)
    input_rows = input_rows.reshape(TRAIN_SEQUENCES, LENGTH, ADAPTER_RANK)
    grads_in = cotangent.reshape(TRAIN_SEQUENCES, LENGTH, MODEL_WIDTH)

    def one_example(pair):
        left, right = pair
        grad = jnp.dot(left.T.astype(jnp.float32), right.astype(jnp.float32), preferred_element_type=jnp.float32).astype(jnp.bfloat16)
        return jnp.dot(grad.astype(jnp.float32), project.astype(jnp.float32), preferred_element_type=jnp.float32).reshape(ADAPTER_RANK * PK)
    table = lax.map(one_example, (input_rows, grads_in))
    kernel = jnp.dot(table, table.T, precision=lax.Precision.HIGHEST)
    cross = jnp.dot(queries.astype(jnp.float32), table.T, precision=lax.Precision.HIGHEST)
    shift = 0.5 * jnp.trace(kernel) / TRAIN_SEQUENCES
    damped_system = kernel + shift * jnp.eye(TRAIN_SEQUENCES, dtype=jnp.float32)
    factor = jnp.linalg.cholesky(damped_system)
    solved = solve_factor(factor, cross.T)
    return TRAIN_SEQUENCES * solved.T
```

```python
import functools

import jax
import jax.numpy as jnp
from jax import lax
from jax.experimental import pallas as pl
from jax.experimental.pallas import tpu as pltpu
from jax.sharding import PartitionSpec as P

RANK = 16
PK = 512
SEQS = 64
MESH = pl.DeviceIdType.MESH
HIGHEST = lax.Precision.HIGHEST
F32 = jnp.float32
BF16 = jnp.bfloat16

PARTNERS = ((1, 2), (1, 0), (1, 1), (1, 3), (0, 2), (0, 1), (0, 3))
DOUBLINGS = 7


def doubling_constants():
    t, c = 130.0 / 128.0, []
    for _ in range(DOUBLINGS):
        c.append(2 * t * t / (2 * t * t - 1))
        t = 2 * t * t - 1
    return c


def nt(a, b, precision=None):
    return lax.dot_general(
        a, b, (((1,), (1,)), ((), ())), precision=precision, preferred_element_type=F32
    )


def take(sem, like):
    pltpu.make_async_copy(like, like, sem).wait()


def kernel(
    acts, cot, down, proj, queries, out,
    acts_v, cot_v, down_v, proj_v, q_v,
    send1, recv1, send2, recv2, parts, send3, recv3, table,
    send_k, recv_k, send_c, recv_c, rows,
    load_sem, acts_sem, s_sem, r_sem,
):
    dp, me = lax.axis_index("dp"), lax.axis_index("tensor")
    x, y = me // 4, lax.rem(me, 4)
    core, spot = lax.rem(dp, 2), dp // 2
    sibling = dp + 1 - 2 * core

    def partner(dx, dy):
        return lax.rem(x + dx, 2) * 4 + lax.rem(y + dy, 4)

    def post(src, dst, stage, device):
        copy = pltpu.make_async_remote_copy(
            src_ref=src, dst_ref=dst, send_sem=s_sem.at[stage], recv_sem=r_sem.at[stage],
            device_id=device, device_id_type=MESH,
        )
        copy.start()

    loads = []

    def load(src, dst, sem):
        copy = pltpu.make_async_copy(src, dst, sem)
        copy.start()
        return copy

    order = [partner(dx, dy) for dx, dy in PARTNERS] + [me]
    down_copy = load(down, down_v, load_sem.at[0])
    acts_copies = []
    for i, p in enumerate(order):
        tokens = pl.ds(pl.multiple_of(p * 256, 256), 256)
        acts_copies.append(load(acts.at[tokens], acts_v.at[i], acts_sem.at[i]))
    for i in range(4):
        tokens = pl.ds(i * 64, 64)
        load(cot.at[tokens], cot_v.at[tokens], load_sem.at[1])
    proj_copy = load(proj, proj_v, load_sem.at[2])
    q_copy = load(queries, q_v, load_sem.at[3])

    barrier = pltpu.get_barrier_semaphore()
    for p in order[:-1]:
        pl.semaphore_signal(barrier, inc=1, device_id={"tensor": p}, device_id_type=MESH)
    pl.semaphore_signal(barrier, inc=1, device_id={"dp": sibling}, device_id_type=MESH)
    for k in range(1, 16):
        there = lax.rem(spot + k, 16) * 2 + core
        pl.semaphore_signal(barrier, inc=1, device_id={"dp": there}, device_id_type=MESH)

    down_copy.wait()
    down_t = down_v[...]
    for i, p in enumerate(order):
        acts_copies[i].wait()
        part = nt(down_t, acts_v[i])
        if i == 0:
            pl.semaphore_wait(barrier, 23)
        if i < 7:
            send1[i] = part
            post(send1.at[i], recv1.at[me], 0, {"tensor": p})
        else:
            recv1[me] = part
    take(r_sem.at[0], recv1.at[pl.ds(0, 7)])
    inputs = recv1[0]
    for t in range(1, 8):
        inputs = inputs + recv1[t]
    inputs = inputs.astype(BF16)

    take(load_sem.at[1], cot_v)
    own_rows = pl.ds(pl.multiple_of(me * 16, 16), 16)
    for i, p in enumerate(order):
        features = pl.ds(pl.multiple_of(p * 1024, 1024), 1024)
        grad = jnp.dot(inputs, cot_v[:, features], preferred_element_type=F32).astype(BF16)
        if i < 7:
            send2[i] = grad
            post(send2.at[i], recv2.at[own_rows], 1, {"tensor": p})
        else:
            recv2[own_rows, :] = grad
    proj_copy.wait()
    take(r_sem.at[1], recv2.at[pl.ds(0, 112)])

    projected = jnp.dot(recv2[...], proj_v[...], preferred_element_type=F32)
    for s in range(2):
        total = projected[64 * s:64 * s + 16]
        for t in range(1, 4):
            total = total + projected[64 * s + 16 * t:64 * s + 16 * t + 16]
        for q in range(4):
            parts[32 * q + 16 * s:32 * q + 16 * s + 16, :] = total[:, 128 * q:128 * q + 128]
    for s in range(2):
        for i in range(2):
            for q in range(4):
                send3[pl.ds(s * 8 + i * 4 + q, 8, stride=16), :] = parts[
                    pl.ds(32 * q + 16 * s + i, 8, stride=2), :
                ]
    for i, p in enumerate(order[:-1]):
        block = pl.ds(pl.multiple_of(p * 16, 16), 16)
        post(send3.at[block], recv3.at[me], 2, {"tensor": p})
    recv3[me] = send3[pl.ds(pl.multiple_of(me * 16, 16), 16), :]
    take(r_sem.at[2], recv3.at[pl.ds(0, 7)])
    mine = recv3[0]
    for t in range(1, 8):
        mine = mine + recv3[t]

    slot = pl.ds(pl.multiple_of(core * 256 + spot * 16, 16), 16)
    table[slot, :] = mine
    for k in range(1, 16):
        there = lax.rem(spot + k, 16) * 2 + core
        post(table.at[slot], table.at[slot], 3, {"dp": there})
    take(r_sem.at[3], table.at[pl.ds(0, 240)])
    half = pl.ds(pl.multiple_of(core * 256, 256), 256)
    post(table.at[half], table.at[half], 4, {"dp": sibling})
    q_copy.wait()
    take(r_sem.at[4], table.at[pl.ds(0, 256)])

    acc = None
    for i in range(4):
        pieces = [table[pl.ds(2 * i + j, 64, stride=8), :] for j in range(2)]
        rows_f = jnp.concatenate(pieces, axis=1)
        hi = rows_f.astype(BF16)
        lo = (rows_f - hi.astype(F32)).astype(BF16)
        both = jnp.concatenate([hi, lo], axis=0)
        right = jnp.concatenate([both, q_v[:, pl.ds(i * 256, 256)]], axis=0)
        term = nt(both, right)
        acc = term if acc is None else acc + term
    acc = acc[:64] + acc[64:]
    gram = acc[:, :128]
    gram = gram + pltpu.roll(gram, 64, 1)
    lane = lax.broadcasted_iota(jnp.int32, (32, 128), 1)
    gram = jnp.where(lane < 64, gram[:32], gram[32:])
    send_k[...] = gram
    for p in order[:-1]:
        post(send_k, recv_k.at[me], 5, {"tensor": p})
    send_c[...] = acc[:, 128:]
    for p in order[:-1]:
        post(send_c, recv_c.at[me], 6, {"tensor": p})
    recv_k[me] = gram
    recv_c[me] = acc[:, 128:]

    take(r_sem.at[5], recv_k.at[pl.ds(0, 7)])
    gram = recv_k[0]
    for t in range(1, 8):
        gram = gram + recv_k[t]
    gram = jnp.concatenate([gram, pltpu.roll(gram, 64, 1)], axis=0)[:, :64]
    eye = (
        lax.broadcasted_iota(jnp.int32, (64, 64), 0)
        == lax.broadcasted_iota(jnp.int32, (64, 64), 1)
    ).astype(F32)
    trace = jnp.sum(gram * eye, keepdims=True)
    unit = 128.0 / (65.0 * trace)
    w = (1.0 - 1.0 / 65.0) * eye - gram * unit
    inverse = eye + w
    scale = 64.0
    constants = doubling_constants()
    for j in range(DOUBLINGS):
        scale = scale * constants[j]
        if j:
            inverse = inverse + jnp.dot(inverse, w, precision=HIGHEST, preferred_element_type=F32)
        if j < DOUBLINGS - 1:
            square = jnp.dot(w, w, precision=HIGHEST, preferred_element_type=F32)
            w = constants[j] * square - (constants[j] - 1.0) * eye

    take(r_sem.at[6], recv_c.at[pl.ds(0, 7)])
    cross = recv_c[0]
    for t in range(1, 8):
        cross = cross + recv_c[t]
    cross = cross * (unit * scale)
    rows[...] = jnp.dot(inverse, cross, precision=HIGHEST, preferred_element_type=F32)
    pieces = []
    for c in range(2):
        for s in range(2):
            pieces.append(rows[pl.ds(c * 32 + s, 16, stride=2), :])
    for c in range(2):
        for s in range(2):
            out[pl.ds(c * 2 + s, 16, stride=4), :] = pieces[c * 2 + s]

    take(s_sem.at[0], send1.at[pl.ds(0, 7)])
    take(s_sem.at[1], send2.at[pl.ds(0, 7)])
    take(s_sem.at[2], send3.at[pl.ds(0, 112)])
    take(s_sem.at[3], table.at[pl.ds(0, 240)])
    take(s_sem.at[4], table.at[pl.ds(0, 256)])
    take(s_sem.at[5], recv_k.at[pl.ds(0, 7)])
    take(s_sem.at[6], recv_c.at[pl.ds(0, 7)])


def shards(acts, cotangent, down_weight, project, queries):
    v = pltpu.VMEM
    scores = pl.pallas_call(
        kernel,
        out_shape=jax.ShapeDtypeStruct((64, 128), F32),
        in_specs=[pl.BlockSpec(memory_space=pl.ANY)] * 5,
        out_specs=pl.BlockSpec(memory_space=pltpu.VMEM),
        scratch_shapes=[
            v((8, 256, 1024), BF16), v((256, 8192), BF16), v((16, 1024), BF16),
            v((1024, 512), BF16), v((128, 1024), BF16),
            v((8, 16, 256), F32), v((8, 16, 256), F32),
            v((8, 16, 1024), BF16), v((128, 1024), BF16),
            v((128, 128), F32), v((128, 128), F32), v((8, 16, 128), F32), v((512, 128), F32),
            v((32, 128), F32), v((8, 32, 128), F32), v((64, 128), F32), v((8, 64, 128), F32),
            v((64, 128), F32),
            pltpu.SemaphoreType.DMA((4,)), pltpu.SemaphoreType.DMA((8,)),
            pltpu.SemaphoreType.DMA((7,)), pltpu.SemaphoreType.DMA((7,)),
        ],
        compiler_params=pltpu.CompilerParams(
            collective_id=0, has_side_effects=True, vmem_limit_bytes=56 * 1024 * 1024
        ),
    )(acts, cotangent, down_weight.T, project, queries)
    return scores.T


def solution(mesh):
    placed = (
        P("dp", "tensor"),
        P(("dp", "tensor"), None),
        P("tensor", None),
        P("tensor", None),
        P("dp", "tensor"),
    )
    return jax.shard_map(
        shards, mesh=mesh, in_specs=placed, out_specs=P("dp", None), check_vma=False
    )
```

```python
import functools

import jax
import jax.numpy as jnp
from jax import lax
from jax.experimental import pallas as pl
from jax.experimental.pallas import tpu as pltpu
from jax.sharding import PartitionSpec as P

RANK = 16
PK = 512
SEQS = 64
MESH = pl.DeviceIdType.MESH
HIGHEST = lax.Precision.HIGHEST
F32 = jnp.float32
BF16 = jnp.bfloat16

PARTNERS = ((1, 2), (1, 1), (1, 3), (0, 2), (1, 0), (0, 1), (0, 3))
AWAY = (14, 13, 15, 12, 4, 11, 8, 3, 5, 10, 9, 2, 6, 1, 7)
NEAR = 12
DOUBLINGS = 7


def doubling_constants():
    t, c = 130.0 / 128.0, []
    for _ in range(DOUBLINGS):
        c.append(2 * t * t / (2 * t * t - 1))
        t = 2 * t * t - 1
    return c


def nt(a, b, precision=None):
    return lax.dot_general(
        a, b, (((1,), (1,)), ((), ())), precision=precision, preferred_element_type=F32
    )


def start(other, e):
    if e < NEAR:
        return 16 * (other * NEAR + e)
    return 16 * (2 * NEAR + other * (16 - NEAR) + e - NEAR)


def take(sem, like):
    pltpu.make_async_copy(like, like, sem).wait()


def kernel(
    acts, cot, down, proj, queries, out,
    acts_v, cot_v, down_v, proj_v, q_v,
    send1, recv1, send2, recv2, parts, send3, recv3, table,
    send_k, recv_k, send_c, recv_c,
    load_sem, acts_sem, s_sem, r_sem, relay,
):
    dp, me = lax.axis_index("dp"), lax.axis_index("tensor")
    x, y = me // 4, lax.rem(me, 4)
    core, spot = lax.rem(dp, 2), dp // 2
    sibling = dp + 1 - 2 * core

    def partner(dx, dy):
        return lax.rem(x + dx, 2) * 4 + lax.rem(y + dy, 4)

    def along(dx, dz):
        return lax.rem(spot // 8 + dx, 2) * 16 + lax.rem(spot + dz, 8) * 2 + core

    def post(src, dst, stage, device):
        copy = pltpu.make_async_remote_copy(
            src_ref=src, dst_ref=dst, send_sem=s_sem.at[stage], recv_sem=r_sem.at[stage],
            device_id=device, device_id_type=MESH,
        )
        copy.start()

    loads = []

    def load(src, dst, sem):
        copy = pltpu.make_async_copy(src, dst, sem)
        copy.start()
        return copy

    order = [partner(dx, dy) for dx, dy in PARTNERS] + [me]
    down_copy = load(down, down_v, load_sem.at[0])
    acts_copies = []

    def load_acts(i):
        tokens = pl.ds(pl.multiple_of(order[i] * 256, 256), 256)
        acts_copies.append(load(acts.at[tokens], acts_v.at[pl.ds(i * 256, 256)], acts_sem.at[i]))

    for i in range(4):
        load_acts(i)

    barrier = pltpu.get_barrier_semaphore()
    for p in order[:-1]:
        pl.semaphore_signal(barrier, inc=1, device_id={"tensor": p}, device_id_type=MESH)
    pl.semaphore_signal(barrier, inc=1, device_id={"dp": sibling}, device_id_type=MESH)
    close = [along(1, 0)] + [along(0, dz) for dz in (2, 6, 1, 7)]
    for there in close:
        pl.semaphore_signal(barrier, inc=1, device_id={"dp": there}, device_id_type=MESH)

    for i in range(4, 8):
        load_acts(i)

    down_copy.wait()
    down_t = down_v[...]
    for pair in range(4):
        acts_copies[2 * pair].wait()
        acts_copies[2 * pair + 1].wait()
        part = nt(down_t, acts_v[pl.ds(pair * 512, 512), :])
        send1[2 * pair] = part[:, :256]
        if pair < 3:
            send1[2 * pair + 1] = part[:, 256:]
        else:
            recv1[me] = part[:, 256:]
        if pair == 1:
            for i in range(4):
                tokens = pl.ds(i * 64, 64)
                load(cot.at[tokens], cot_v.at[tokens], load_sem.at[1])
            proj_copy = load(proj, proj_v, load_sem.at[2])
            q_copy = load(queries, q_v, load_sem.at[3])
            pl.semaphore_wait(barrier, 13)
            for i in range(2):
                post(send1.at[i], recv1.at[me], 0, {"tensor": order[i]})
        if pair > 0:
            for i in range(2 * pair, min(2 * pair + 2, 7)):
                post(send1.at[i], recv1.at[me], 0, {"tensor": order[i]})
    for dz in (2, 6):
        pl.semaphore_signal(relay.at[0], inc=1, device_id={"dp": along(0, dz)}, device_id_type=MESH)
    take(r_sem.at[0], recv1.at[pl.ds(0, 7)])
    inputs = recv1[0]
    for t in range(1, 8):
        inputs = inputs + recv1[t]
    inputs = inputs.astype(BF16)

    take(load_sem.at[1], cot_v)
    own_rows = pl.ds(pl.multiple_of(me * 16, 16), 16)
    for i, p in enumerate(order):
        features = pl.ds(pl.multiple_of(p * 1024, 1024), 1024)
        grad = jnp.dot(inputs, cot_v[:, features], preferred_element_type=F32).astype(BF16)
        if i < 7:
            send2[i] = grad
            post(send2.at[i], recv2.at[own_rows], 1, {"tensor": p})
        else:
            recv2[own_rows, :] = grad
    pl.semaphore_wait(relay.at[0], 2)
    pl.semaphore_signal(relay.at[1], inc=1, device_id={"dp": along(1, 0)}, device_id_type=MESH)
    proj_copy.wait()
    take(r_sem.at[1], recv2.at[pl.ds(0, 112)])

    projected = jnp.dot(recv2[...], proj_v[...], preferred_element_type=F32)
    for s in range(2):
        total = projected[64 * s:64 * s + 16]
        for t in range(1, 4):
            total = total + projected[64 * s + 16 * t:64 * s + 16 * t + 16]
        for q in range(4):
            parts[32 * q + 16 * s:32 * q + 16 * s + 16, :] = total[:, 128 * q:128 * q + 128]
    for s in range(2):
        for i in range(2):
            for q in range(4):
                send3[pl.ds(s * 8 + i * 4 + q, 8, stride=16), :] = parts[
                    pl.ds(32 * q + 16 * s + i, 8, stride=2), :
                ]
    for i, p in enumerate(order[:-1]):
        block = pl.ds(pl.multiple_of(p * 16, 16), 16)
        post(send3.at[block], recv3.at[me], 2, {"tensor": p})
    recv3[me] = send3[pl.ds(pl.multiple_of(me * 16, 16), 16), :]
    take(r_sem.at[2], recv3.at[pl.ds(0, 7)])
    mine = recv3[0]
    for t in range(1, 8):
        mine = mine + recv3[t]

    table[0:16, :] = mine
    pl.semaphore_wait(relay.at[1], 1)
    for e in AWAY:
        back = 8 - e if e < 8 else 8 + (20 - e) % 8
        there = along(e // 8, (e - 2 * (e // 8)) % 8)
        block = table.at[pl.ds(start(0, back), 16)]
        post(table.at[pl.ds(0, 16)], block, 3 if back >= NEAR else 4, {"dp": there})
    take(r_sem.at[4], table.at[pl.ds(0, 16 * (NEAR - 1))])
    near = pl.ds(0, 16 * NEAR)
    post(table.at[near], table.at[pl.ds(start(1, 0), 16 * NEAR)], 7, {"dp": sibling})
    q_copy.wait()
    take(r_sem.at[3], table.at[pl.ds(0, 16 * (16 - NEAR))])
    far = pl.ds(start(0, NEAR), 16 * (16 - NEAR))
    post(table.at[far], table.at[pl.ds(start(1, NEAR), 16 * (16 - NEAR))], 8, {"dp": sibling})
    take(r_sem.at[7], table.at[near])
    take(r_sem.at[8], table.at[far])

    acc = None
    for i in range(4):
        pieces = [table[pl.ds(2 * i + j, 64, stride=8), :] for j in range(2)]
        rows_f = jnp.concatenate(pieces, axis=1)
        hi = rows_f.astype(BF16)
        lo = (rows_f - hi.astype(F32)).astype(BF16)
        both = jnp.concatenate([hi, lo], axis=0)
        right = jnp.concatenate([both, q_v[:, pl.ds(i * 256, 256)]], axis=0)
        term = nt(both, right)
        acc = term if acc is None else acc + term
    acc = acc[:64] + acc[64:]
    gram = acc[:, :128]
    gram = gram + pltpu.roll(gram, 64, 1)
    lane = lax.broadcasted_iota(jnp.int32, (32, 128), 1)
    gram = jnp.where(lane < 64, gram[:32], gram[32:])
    send_k[...] = gram
    for p in order[:-1]:
        post(send_k, recv_k.at[me], 5, {"tensor": p})
    send_c[...] = acc[:, 128:].astype(BF16)
    for p in order[:-1]:
        post(send_c, recv_c.at[me], 6, {"tensor": p})
    recv_k[me] = gram
    recv_c[me] = acc[:, 128:].astype(BF16)

    take(r_sem.at[5], recv_k.at[pl.ds(0, 7)])
    gram = recv_k[0]
    for t in range(1, 8):
        gram = gram + recv_k[t]
    gram = jnp.concatenate([gram, pltpu.roll(gram, 64, 1)], axis=0)[:, :64]
    eye = (
        lax.broadcasted_iota(jnp.int32, (64, 64), 0)
        == lax.broadcasted_iota(jnp.int32, (64, 64), 1)
    ).astype(F32)
    trace = jnp.sum(gram * eye, keepdims=True)
    unit = 128.0 / (65.0 * trace)
    w = (1.0 - 1.0 / 65.0) * eye - gram * unit
    inverse = eye + w
    row = lax.broadcasted_iota(jnp.int32, (64, 64), 0)
    column = lax.broadcasted_iota(jnp.int32, (64, 64), 1)
    block = column // 2
    near_block = block < 2 * NEAR
    other = jnp.where(near_block, block // NEAR, (block - 2 * NEAR) // (16 - NEAR))
    e = jnp.where(near_block, lax.rem(block, NEAR), NEAR + lax.rem(block, 16 - NEAR))
    dx = e // 8
    place = lax.rem(spot // 8 + dx, 2) * 32 + lax.rem(lax.rem(spot, 8) + e - 2 * dx + 8, 8) * 4
    place = place + lax.rem(core + other, 2) * 2 + lax.rem(column, 2)
    place = (place == row).astype(F32)
    scale = 64.0
    constants = doubling_constants()
    for j in range(DOUBLINGS):
        scale = scale * constants[j]
        if j:
            inverse = inverse + jnp.dot(inverse, w, precision=lax.Precision.HIGH, preferred_element_type=F32)
        if j < DOUBLINGS - 1:
            square = jnp.dot(w, w, precision=lax.Precision.HIGH, preferred_element_type=F32)
            w = constants[j] * square - (constants[j] - 1.0) * eye

    inverse = jnp.dot(place, inverse * (unit * scale), precision=lax.Precision.HIGH, preferred_element_type=F32)

    take(r_sem.at[6], recv_c.at[pl.ds(0, 7)])
    cross = recv_c[0].astype(F32)
    for t in range(1, 8):
        cross = cross + recv_c[t].astype(F32)
    out[...] = jnp.dot(inverse, cross, precision=lax.Precision.HIGH, preferred_element_type=F32)

    take(s_sem.at[0], send1.at[pl.ds(0, 7)])
    take(s_sem.at[1], send2.at[pl.ds(0, 7)])
    take(s_sem.at[2], send3.at[pl.ds(0, 112)])
    take(s_sem.at[3], table.at[pl.ds(0, 16 * (16 - NEAR))])
    take(s_sem.at[4], table.at[pl.ds(0, 16 * (NEAR - 1))])
    take(s_sem.at[5], recv_k.at[pl.ds(0, 7)])
    take(s_sem.at[6], recv_c.at[pl.ds(0, 7)])
    take(s_sem.at[7], table.at[near])
    take(s_sem.at[8], table.at[far])


def shards(acts, cotangent, down_weight, project, queries):
    v = pltpu.VMEM
    scores = pl.pallas_call(
        kernel,
        out_shape=pltpu.VMEM((64, 128), F32),
        in_specs=[pl.BlockSpec(memory_space=pl.ANY)] * 5,
        out_specs=pl.BlockSpec(memory_space=pltpu.VMEM),
        scratch_shapes=[
            v((2048, 1024), BF16), v((256, 8192), BF16), v((16, 1024), BF16),
            v((1024, 512), BF16), v((128, 1024), BF16),
            v((8, 16, 256), F32), v((8, 16, 256), F32),
            v((8, 16, 1024), BF16), v((128, 1024), BF16),
            v((128, 128), F32), v((128, 128), F32), v((8, 16, 128), F32), v((512, 128), F32),
            v((32, 128), F32), v((8, 32, 128), F32), v((64, 128), BF16), v((8, 64, 128), BF16),
            pltpu.SemaphoreType.DMA((4,)), pltpu.SemaphoreType.DMA((8,)),
            pltpu.SemaphoreType.DMA((9,)), pltpu.SemaphoreType.DMA((9,)),
            pltpu.SemaphoreType.REGULAR((2,)),
        ],
        compiler_params=pltpu.CompilerParams(
            collective_id=0, has_side_effects=True, vmem_limit_bytes=56 * 1024 * 1024
        ),
    )(acts, cotangent, down_weight.T, project, queries)
    return scores.T


def solution(mesh):
    placed = (
        P("dp", "tensor"),
        P(("dp", "tensor"), None),
        P("tensor", None),
        P("tensor", None),
        P("dp", "tensor"),
    )
    return jax.shard_map(
        shards, mesh=mesh, in_specs=placed, out_specs=P("dp", None), check_vma=False
    )
```

```python
import functools

import jax
import jax.numpy as jnp
from jax import lax
from jax.experimental import pallas as pl
from jax.experimental.pallas import tpu as pltpu
from jax.sharding import PartitionSpec as P

RANK = 16
PK = 512
SEQS = 64
MESH = pl.DeviceIdType.MESH
F32 = jnp.float32
BF16 = jnp.bfloat16

PARTNERS = ((1, 2), (1, 1), (1, 3), (0, 2), (1, 0), (0, 1), (0, 3))
AWAY = (14, 13, 15, 12, 4, 11, 8, 3, 5, 10, 9, 2, 6, 1, 7)
NEAR = 13
DOUBLINGS = 7


def doubling_constants():
    t, c = 130.0 / 128.0, []
    for _ in range(DOUBLINGS):
        c.append(2 * t * t / (2 * t * t - 1))
        t = 2 * t * t - 1
    return c


def nt(a, b):
    return lax.dot_general(
        a, b, (((1,), (1,)), ((), ())), preferred_element_type=F32
    )


def start(other, e):
    if e < NEAR:
        return 16 * (other * NEAR + e)
    return 16 * (2 * NEAR + other * (16 - NEAR) + e - NEAR)


def split(a):
    high = a.astype(BF16)
    return high, (a - high.astype(F32)).astype(BF16)


def product(lefts, right):
    rows = []
    for left in lefts:
        high, low = split(left)
        lane = lax.broadcasted_iota(jnp.int32, left.shape, 1)
        rows.append(jnp.where(lane < 64, high, low))
    left = jnp.concatenate(rows, axis=0)
    high, low = split(right)
    return jnp.dot(
        jnp.concatenate([left, left], axis=1),
        jnp.concatenate([high, high, low, low], axis=0),
        preferred_element_type=F32,
    )


def take(sem, like):
    pltpu.make_async_copy(like, like, sem).wait()


def kernel(
    acts, cot, down, proj, queries, out,
    acts_v, cot_v, down_v, proj_v, q_v,
    send1, recv1, send2, recv2, parts, send3, recv3, table, wide,
    send_k, recv_k, send_c, recv_c,
    load_sem, acts_sem, s_sem, r_sem, relay,
):
    dp, me = lax.axis_index("dp"), lax.axis_index("tensor")
    x, y = me // 4, lax.rem(me, 4)
    core, spot = lax.rem(dp, 2), dp // 2
    sibling = dp + 1 - 2 * core

    def partner(dx, dy):
        return lax.rem(x + dx, 2) * 4 + lax.rem(y + dy, 4)

    def along(dx, dz):
        return lax.rem(spot // 8 + dx, 2) * 16 + lax.rem(spot + dz, 8) * 2 + core

    def post(src, dst, stage, device):
        copy = pltpu.make_async_remote_copy(
            src_ref=src, dst_ref=dst, send_sem=s_sem.at[stage], recv_sem=r_sem.at[stage],
            device_id=device, device_id_type=MESH,
        )
        copy.start()

    loads = []

    def load(src, dst, sem):
        copy = pltpu.make_async_copy(src, dst, sem)
        copy.start()
        return copy

    order = [partner(dx, dy) for dx, dy in PARTNERS] + [me]
    down_copy = load(down, down_v, load_sem.at[0])
    acts_copies = []

    def load_acts(i):
        tokens = pl.ds(pl.multiple_of(order[i] * 256, 256), 256)
        acts_copies.append(load(acts.at[tokens], acts_v.at[pl.ds(i * 256, 256)], acts_sem.at[i]))

    for i in range(4):
        load_acts(i)

    barrier = pltpu.get_barrier_semaphore()
    for p in order[:-1]:
        pl.semaphore_signal(barrier, inc=1, device_id={"tensor": p}, device_id_type=MESH)
    pl.semaphore_signal(barrier, inc=1, device_id={"dp": sibling}, device_id_type=MESH)
    close = [along(1, 0)] + [along(0, dz) for dz in (2, 6, 1, 7)]
    for there in close:
        pl.semaphore_signal(barrier, inc=1, device_id={"dp": there}, device_id_type=MESH)

    for i in range(4, 8):
        load_acts(i)

    down_copy.wait()
    down_t = down_v[...]
    for pair in range(4):
        acts_copies[2 * pair].wait()
        acts_copies[2 * pair + 1].wait()
        part = nt(down_t, acts_v[pl.ds(pair * 512, 512), :])
        send1[2 * pair] = part[:, :256]
        if pair < 3:
            send1[2 * pair + 1] = part[:, 256:]
        else:
            recv1[me] = part[:, 256:]
        if pair == 1:
            for i in range(4):
                tokens = pl.ds(i * 64, 64)
                load(cot.at[tokens], cot_v.at[tokens], load_sem.at[1])
            proj_copy = load(proj, proj_v, load_sem.at[2])
            q_copy = load(queries, q_v, load_sem.at[3])
            pl.semaphore_wait(barrier, 13)
            for i in range(2):
                post(send1.at[i], recv1.at[me], 0, {"tensor": order[i]})
        if pair > 0:
            for i in range(2 * pair, min(2 * pair + 2, 7)):
                post(send1.at[i], recv1.at[me], 0, {"tensor": order[i]})
    for dz in (2, 6):
        pl.semaphore_signal(relay.at[0], inc=1, device_id={"dp": along(0, dz)}, device_id_type=MESH)
    take(r_sem.at[0], recv1.at[pl.ds(0, 7)])
    inputs = recv1[0]
    for t in range(1, 8):
        inputs = inputs + recv1[t]
    inputs = inputs.astype(BF16)

    take(load_sem.at[1], cot_v)
    own_rows = pl.ds(pl.multiple_of(me * 16, 16), 16)
    for i, p in enumerate(order):
        features = pl.ds(pl.multiple_of(p * 1024, 1024), 1024)
        grad = jnp.dot(inputs, cot_v[:, features], preferred_element_type=F32).astype(BF16)
        if i < 7:
            send2[i] = grad
            post(send2.at[i], recv2.at[own_rows], 1, {"tensor": p})
        else:
            recv2[own_rows, :] = grad
    pl.semaphore_wait(relay.at[0], 2)
    pl.semaphore_signal(relay.at[1], inc=1, device_id={"dp": along(1, 0)}, device_id_type=MESH)
    pl.semaphore_wait(relay.at[1], 1)
    pl.semaphore_signal(relay.at[2], inc=1, device_id={"dp": sibling}, device_id_type=MESH)
    proj_copy.wait()
    take(r_sem.at[1], recv2.at[pl.ds(0, 112)])

    projected = jnp.dot(recv2[...], proj_v[...], preferred_element_type=F32)
    for s in range(2):
        total = projected[64 * s:64 * s + 16]
        for t in range(1, 4):
            total = total + projected[64 * s + 16 * t:64 * s + 16 * t + 16]
        for q in range(4):
            parts[32 * q + 16 * s:32 * q + 16 * s + 16, :] = total[:, 128 * q:128 * q + 128]
    for s in range(2):
        for i in range(2):
            for q in range(4):
                send3[pl.ds(s * 8 + i * 4 + q, 8, stride=16), :] = parts[
                    pl.ds(32 * q + 16 * s + i, 8, stride=2), :
                ]
    for i, p in enumerate(order[:-1]):
        block = pl.ds(pl.multiple_of(p * 16, 16), 16)
        post(send3.at[block], recv3.at[me], 2, {"tensor": p})
    recv3[me] = send3[pl.ds(pl.multiple_of(me * 16, 16), 16), :]
    take(r_sem.at[2], recv3.at[pl.ds(0, 7)])
    mine = recv3[0]
    for t in range(1, 8):
        mine = mine + recv3[t]

    table[0:16, :] = mine.astype(BF16)
    pl.semaphore_wait(relay.at[2], 1)
    for e in AWAY:
        back = 8 - e if e < 8 else 8 + (20 - e) % 8
        there = along(e // 8, (e - 2 * (e // 8)) % 8)
        own = table.at[pl.ds(0, 16)]
        post(own, table.at[pl.ds(start(0, back), 16)], 3 if e >= NEAR else 4, {"dp": there})
        if e >= NEAR:
            post(own, table.at[pl.ds(start(1, back), 16)], 3, {"dp": there + 1 - 2 * core})
    take(r_sem.at[4], table.at[pl.ds(0, 16 * (NEAR - 1))])
    near = pl.ds(0, 16 * NEAR)
    post(table.at[near], table.at[pl.ds(start(1, 0), 16 * NEAR)], 7, {"dp": sibling})
    q_copy.wait()
    take(r_sem.at[7], table.at[near])
    both_near, far = pl.ds(0, 32 * NEAR), pl.ds(32 * NEAR, 32 * (16 - NEAR))
    wide[both_near, :] = table[both_near, :].astype(F32)
    take(r_sem.at[3], table.at[far])
    wide[far, :] = table[far, :].astype(F32)

    pieces = [wide[pl.ds(j, 64, stride=8), :].astype(BF16) for j in range(8)]
    whole = jnp.concatenate(pieces, axis=1)
    acc = nt(whole, jnp.concatenate([whole, whole, q_v[...]], axis=0))
    gram = acc[:, :128]
    lane = lax.broadcasted_iota(jnp.int32, (32, 128), 1)
    gram = jnp.where(lane < 64, gram[:32], gram[32:])
    send_k[...] = gram
    for p in order[:-1]:
        post(send_k, recv_k.at[me], 5, {"tensor": p})
    send_c[...] = acc[:, 128:].astype(BF16)
    for p in order[:-1]:
        post(send_c, recv_c.at[me], 6, {"tensor": p})
    recv_k[me] = gram
    recv_c[me] = acc[:, 128:].astype(BF16)

    take(r_sem.at[5], recv_k.at[pl.ds(0, 7)])
    gram = recv_k[0]
    for t in range(1, 8):
        gram = gram + recv_k[t]
    turned = pltpu.roll(gram, 64, 1)
    gram = jnp.concatenate(
        [jnp.where(lane < 64, gram, turned), jnp.where(lane < 64, turned, gram)], axis=0
    )
    row = lax.broadcasted_iota(jnp.int32, (64, 128), 0)
    column = lax.rem(lax.broadcasted_iota(jnp.int32, (64, 128), 1), 64)
    eye = (row == column).astype(F32)
    unit = 256.0 / (65.0 * jnp.sum(gram * eye, keepdims=True))
    w = (1.0 - 1.0 / 65.0) * eye - gram * unit
    block = column // 2
    near_block = block < 2 * NEAR
    other = jnp.where(near_block, block // NEAR, (block - 2 * NEAR) // (16 - NEAR))
    e = jnp.where(
        near_block, lax.rem(block, NEAR), NEAR + lax.rem(block - 2 * NEAR + 16 - NEAR, 16 - NEAR)
    )
    dx = e // 8
    place = lax.rem(spot // 8 + dx, 2) * 32 + lax.rem(lax.rem(spot, 8) + e - 2 * dx + 8, 8) * 4
    place = place + lax.rem(core + other, 2) * 2 + lax.rem(column, 2)
    place = (place == row).astype(F32)
    inverse = place
    scale = 64.0
    constants = doubling_constants()
    for j in range(DOUBLINGS):
        scale = scale * constants[j]
        if j < DOUBLINGS - 1:
            products = product([w, inverse], w)
            inverse = inverse + products[64:]
            w = constants[j] * products[:64] - (constants[j] - 1.0) * eye
        else:
            inverse = inverse + product([inverse], w)
    inverse = inverse * (unit * scale)

    take(r_sem.at[6], recv_c.at[pl.ds(0, 7)])
    cross = recv_c[0].astype(F32)
    for t in range(1, 8):
        cross = cross + recv_c[t].astype(F32)
    out[...] = product([inverse], cross)

    take(s_sem.at[0], send1.at[pl.ds(0, 7)])
    take(s_sem.at[1], send2.at[pl.ds(0, 7)])
    take(s_sem.at[2], send3.at[pl.ds(0, 112)])
    take(s_sem.at[3], table.at[far])
    take(s_sem.at[4], table.at[pl.ds(0, 16 * (NEAR - 1))])
    take(s_sem.at[5], recv_k.at[pl.ds(0, 7)])
    take(s_sem.at[6], recv_c.at[pl.ds(0, 7)])
    take(s_sem.at[7], table.at[near])


def shards(acts, cotangent, down_weight, project, queries):
    v = pltpu.VMEM
    scores = pl.pallas_call(
        kernel,
        out_shape=pltpu.VMEM((64, 128), F32),
        in_specs=[pl.BlockSpec(memory_space=pl.ANY)] * 5,
        out_specs=pl.BlockSpec(memory_space=pltpu.VMEM),
        scratch_shapes=[
            v((2048, 1024), BF16), v((256, 8192), BF16), v((16, 1024), BF16),
            v((1024, 512), BF16), v((128, 1024), BF16),
            v((8, 16, 256), F32), v((8, 16, 256), F32),
            v((8, 16, 1024), BF16), v((128, 1024), BF16),
            v((128, 128), F32), v((128, 128), F32), v((8, 16, 128), F32), v((512, 128), BF16), v((512, 128), F32),
            v((32, 128), F32), v((8, 32, 128), F32), v((64, 128), BF16), v((8, 64, 128), BF16),
            pltpu.SemaphoreType.DMA((4,)), pltpu.SemaphoreType.DMA((8,)),
            pltpu.SemaphoreType.DMA((8,)), pltpu.SemaphoreType.DMA((8,)),
            pltpu.SemaphoreType.REGULAR((3,)),
        ],
        compiler_params=pltpu.CompilerParams(
            collective_id=0, has_side_effects=True, vmem_limit_bytes=56 * 1024 * 1024
        ),
    )(acts, cotangent, down_weight.T, project, queries)
    return scores.T


def solution(mesh):
    placed = (
        P("dp", "tensor"),
        P(("dp", "tensor"), None),
        P("tensor", None),
        P("tensor", None),
        P("dp", "tensor"),
    )
    return jax.shard_map(
        shards, mesh=mesh, in_specs=placed, out_specs=P("dp", None), check_vma=False
    )
```

```python
import functools

import jax
import jax.numpy as jnp
from jax import lax
from jax.experimental import pallas as pl
from jax.experimental.pallas import tpu as pltpu
from jax.sharding import PartitionSpec as P

RANK = 16
PK = 512
SEQS = 64
MESH = pl.DeviceIdType.MESH
F32 = jnp.float32
BF16 = jnp.bfloat16

PARTNERS = ((1, 2), (0, 2), (1, 1), (1, 3), (0, 1), (1, 0), (0, 3))
AWAY = (14, 13, 15, 12, 4, 11, 8, 3, 5, 10, 9, 2, 6, 1, 7)
NEAR = 13
DOUBLINGS = 7


def doubling_constants():
    t, c = 130.0 / 128.0, []
    for _ in range(DOUBLINGS):
        c.append(2 * t * t / (2 * t * t - 1))
        t = 2 * t * t - 1
    return c


def nt(a, b):
    return lax.dot_general(
        a, b, (((1,), (1,)), ((), ())), preferred_element_type=F32
    )


def start(other, e):
    if e < NEAR:
        return 16 * (other * NEAR + e)
    return 16 * (2 * NEAR + other * (16 - NEAR) + e - NEAR)


def split(a):
    high = a.astype(BF16)
    return high, (a - high.astype(F32)).astype(BF16)


def product(lefts, right):
    rows = []
    for left in lefts:
        high, low = split(left)
        lane = lax.broadcasted_iota(jnp.int32, left.shape, 1)
        rows.append(jnp.where(lane < 64, high, low))
    left = jnp.concatenate(rows, axis=0)
    high, low = split(right)
    return jnp.dot(
        jnp.concatenate([left, left], axis=1),
        jnp.concatenate([high, high, low, low], axis=0),
        preferred_element_type=F32,
    )


def take(sem, like):
    pltpu.make_async_copy(like, like, sem).wait()


def kernel(
    acts, cot, down, proj, queries, out,
    acts_v, cot_v, down_v, proj_v, q_v,
    send1, recv1, send2, recv2, parts, send3, recv3, table, wide,
    send_k, recv_k, send_c, recv_c,
    load_sem, acts_sem, s_sem, r_sem, relay,
):
    dp, me = lax.axis_index("dp"), lax.axis_index("tensor")
    x, y = me // 4, lax.rem(me, 4)
    core, spot = lax.rem(dp, 2), dp // 2
    sibling = dp + 1 - 2 * core

    def partner(dx, dy):
        return lax.rem(x + dx, 2) * 4 + lax.rem(y + dy, 4)

    def along(dx, dz):
        return lax.rem(spot // 8 + dx, 2) * 16 + lax.rem(spot + dz, 8) * 2 + core

    def post(src, dst, stage, device):
        copy = pltpu.make_async_remote_copy(
            src_ref=src, dst_ref=dst, send_sem=s_sem.at[stage], recv_sem=r_sem.at[stage],
            device_id=device, device_id_type=MESH,
        )
        copy.start()

    loads = []

    def load(src, dst, sem):
        copy = pltpu.make_async_copy(src, dst, sem)
        copy.start()
        return copy

    order = [partner(dx, dy) for dx, dy in PARTNERS] + [me]
    down_copy = load(down, down_v, load_sem.at[0])
    acts_copies = []

    def load_acts(i):
        tokens = pl.ds(pl.multiple_of(order[i] * 256, 256), 256)
        acts_copies.append(load(acts.at[tokens], acts_v.at[pl.ds(i * 256, 256)], acts_sem.at[i]))

    for i in range(4):
        load_acts(i)

    barrier = pltpu.get_barrier_semaphore()
    for p in order[:-1]:
        pl.semaphore_signal(barrier, inc=1, device_id={"tensor": p}, device_id_type=MESH)
    pl.semaphore_signal(barrier, inc=1, device_id={"dp": sibling}, device_id_type=MESH)
    close = [along(1, 0)] + [along(0, dz) for dz in (2, 6, 1, 7)]
    for there in close:
        pl.semaphore_signal(barrier, inc=1, device_id={"dp": there}, device_id_type=MESH)

    for i in range(4, 8):
        load_acts(i)

    down_copy.wait()
    down_t = down_v[...]
    for pair in range(4):
        acts_copies[2 * pair].wait()
        acts_copies[2 * pair + 1].wait()
        part = nt(down_t, acts_v[pl.ds(pair * 512, 512), :])
        send1[2 * pair] = part[:, :256]
        if pair < 3:
            send1[2 * pair + 1] = part[:, 256:]
        else:
            recv1[me] = part[:, 256:]
        if pair == 1:
            for i in range(4):
                tokens = pl.ds(i * 64, 64)
                load(cot.at[tokens], cot_v.at[tokens], load_sem.at[1])
            proj_copy = load(proj, proj_v, load_sem.at[2])
            q_copy = load(queries, q_v, load_sem.at[3])
            pl.semaphore_wait(barrier, 13)
            for i in range(2):
                post(send1.at[i], recv1.at[me], 0, {"tensor": order[i]})
        if pair > 0:
            for i in range(2 * pair, min(2 * pair + 2, 7)):
                post(send1.at[i], recv1.at[me], 0, {"tensor": order[i]})
    for dz in (2, 6):
        pl.semaphore_signal(relay.at[0], inc=1, device_id={"dp": along(0, dz)}, device_id_type=MESH)
    take(r_sem.at[0], recv1.at[pl.ds(0, 7)])
    inputs = recv1[0]
    for t in range(1, 8):
        inputs = inputs + recv1[t]
    inputs = inputs.astype(BF16)

    take(load_sem.at[1], cot_v)
    own_rows = pl.ds(pl.multiple_of(me * 16, 16), 16)
    for i, p in enumerate(order):
        features = pl.ds(pl.multiple_of(p * 1024, 1024), 1024)
        grad = jnp.dot(inputs, cot_v[:, features], preferred_element_type=F32).astype(BF16)
        if i < 7:
            send2[i] = grad
            post(send2.at[i], recv2.at[own_rows], 1, {"tensor": p})
        else:
            recv2[own_rows, :] = grad
    pl.semaphore_wait(relay.at[0], 2)
    pl.semaphore_signal(relay.at[1], inc=1, device_id={"dp": along(1, 0)}, device_id_type=MESH)
    pl.semaphore_wait(relay.at[1], 1)
    pl.semaphore_signal(relay.at[2], inc=1, device_id={"dp": sibling}, device_id_type=MESH)
    proj_copy.wait()
    take(r_sem.at[1], recv2.at[pl.ds(0, 112)])

    projected = jnp.dot(recv2[...], proj_v[...], preferred_element_type=F32)
    for s in range(2):
        total = projected[64 * s:64 * s + 16]
        for t in range(1, 4):
            total = total + projected[64 * s + 16 * t:64 * s + 16 * t + 16]
        for q in range(4):
            parts[32 * q + 16 * s:32 * q + 16 * s + 16, :] = total[:, 128 * q:128 * q + 128]
    for s in range(2):
        for i in range(2):
            for q in range(4):
                send3[pl.ds(s * 8 + i * 4 + q, 8, stride=16), :] = parts[
                    pl.ds(32 * q + 16 * s + i, 8, stride=2), :
                ]
    for i, p in enumerate(order[:-1]):
        block = pl.ds(pl.multiple_of(p * 16, 16), 16)
        post(send3.at[block], recv3.at[me], 2, {"tensor": p})
    recv3[me] = send3[pl.ds(pl.multiple_of(me * 16, 16), 16), :]
    take(r_sem.at[2], recv3.at[pl.ds(0, 7)])
    mine = recv3[0]
    for t in range(1, 8):
        mine = mine + recv3[t]

    table[0:16, :] = mine.astype(BF16)
    pl.semaphore_wait(relay.at[2], 1)
    for e in AWAY:
        back = 8 - e if e < 8 else 8 + (20 - e) % 8
        there = along(e // 8, (e - 2 * (e // 8)) % 8)
        own = table.at[pl.ds(0, 16)]
        post(own, table.at[pl.ds(start(0, back), 16)], 3 if e >= NEAR else 4, {"dp": there})
        if e >= NEAR:
            post(own, table.at[pl.ds(start(1, back), 16)], 3, {"dp": there + 1 - 2 * core})
    take(r_sem.at[4], table.at[pl.ds(0, 16 * (NEAR - 1))])
    near = pl.ds(0, 16 * NEAR)
    post(table.at[near], table.at[pl.ds(start(1, 0), 16 * NEAR)], 7, {"dp": sibling})
    q_copy.wait()
    take(r_sem.at[7], table.at[near])
    both_near, far = pl.ds(0, 32 * NEAR), pl.ds(32 * NEAR, 32 * (16 - NEAR))
    wide[both_near, :] = table[both_near, :].astype(F32)
    take(r_sem.at[3], table.at[far])
    wide[far, :] = table[far, :].astype(F32)

    pieces = [wide[pl.ds(j, 64, stride=8), :].astype(BF16) for j in range(8)]
    whole = jnp.concatenate(pieces, axis=1)
    gram = nt(whole, jnp.concatenate([whole, whole], axis=0))
    lane = lax.broadcasted_iota(jnp.int32, (32, 128), 1)
    gram = jnp.where(lane < 64, gram[:32], gram[32:])
    send_k[...] = gram
    for p in order[:-1]:
        post(send_k, recv_k.at[me], 5, {"tensor": p})
    recv_k[me] = gram
    cross = nt(whole, q_v[...]).astype(BF16)
    send_c[...] = cross
    for p in order[:-1]:
        post(send_c, recv_c.at[me], 6, {"tensor": p})
    recv_c[me] = cross

    take(r_sem.at[5], recv_k.at[pl.ds(0, 7)])
    gram = recv_k[0]
    for t in range(1, 8):
        gram = gram + recv_k[t]
    turned = pltpu.roll(gram, 64, 1)
    gram = jnp.concatenate(
        [jnp.where(lane < 64, gram, turned), jnp.where(lane < 64, turned, gram)], axis=0
    )
    row = lax.broadcasted_iota(jnp.int32, (64, 128), 0)
    column = lax.rem(lax.broadcasted_iota(jnp.int32, (64, 128), 1), 64)
    eye = (row == column).astype(F32)
    unit = 256.0 / (65.0 * jnp.sum(gram * eye, keepdims=True))
    w = (1.0 - 1.0 / 65.0) * eye - gram * unit
    block = column // 2
    near_block = block < 2 * NEAR
    other = jnp.where(near_block, block // NEAR, (block - 2 * NEAR) // (16 - NEAR))
    e = jnp.where(
        near_block, lax.rem(block, NEAR), NEAR + lax.rem(block - 2 * NEAR + 16 - NEAR, 16 - NEAR)
    )
    dx = e // 8
    place = lax.rem(spot // 8 + dx, 2) * 32 + lax.rem(lax.rem(spot, 8) + e - 2 * dx + 8, 8) * 4
    place = place + lax.rem(core + other, 2) * 2 + lax.rem(column, 2)
    place = (place == row).astype(F32)
    inverse = place
    scale = 64.0
    constants = doubling_constants()
    for j in range(DOUBLINGS):
        scale = scale * constants[j]
        if j < DOUBLINGS - 1:
            products = product([w, inverse], w)
            inverse = inverse + products[64:]
            w = constants[j] * products[:64] - (constants[j] - 1.0) * eye
        else:
            inverse = inverse + product([inverse], w)
    inverse = inverse * (unit * scale)

    take(s_sem.at[0], send1.at[pl.ds(0, 7)])
    take(s_sem.at[1], send2.at[pl.ds(0, 7)])
    take(s_sem.at[2], send3.at[pl.ds(0, 112)])
    take(s_sem.at[3], table.at[far])
    take(s_sem.at[4], table.at[pl.ds(0, 16 * (NEAR - 1))])
    take(s_sem.at[7], table.at[near])

    take(r_sem.at[6], recv_c.at[pl.ds(0, 7)])
    cross = recv_c[0].astype(F32)
    for t in range(1, 8):
        cross = cross + recv_c[t].astype(F32)
    out[...] = product([inverse], cross)
    take(s_sem.at[5], recv_k.at[pl.ds(0, 7)])
    take(s_sem.at[6], recv_c.at[pl.ds(0, 7)])


def shards(acts, cotangent, down_weight, project, queries):
    v = pltpu.VMEM
    scores = pl.pallas_call(
        kernel,
        out_shape=pltpu.VMEM((64, 128), F32),
        in_specs=[pl.BlockSpec(memory_space=pl.ANY)] * 5,
        out_specs=pl.BlockSpec(memory_space=pltpu.VMEM),
        scratch_shapes=[
            v((2048, 1024), BF16), v((256, 8192), BF16), v((16, 1024), BF16),
            v((1024, 512), BF16), v((128, 1024), BF16),
            v((8, 16, 256), F32), v((8, 16, 256), F32),
            v((8, 16, 1024), BF16), v((128, 1024), BF16),
            v((128, 128), F32), v((128, 128), F32), v((8, 16, 128), F32), v((512, 128), BF16), v((512, 128), F32),
            v((32, 128), F32), v((8, 32, 128), F32), v((64, 128), BF16), v((8, 64, 128), BF16),
            pltpu.SemaphoreType.DMA((4,)), pltpu.SemaphoreType.DMA((8,)),
            pltpu.SemaphoreType.DMA((8,)), pltpu.SemaphoreType.DMA((8,)),
            pltpu.SemaphoreType.REGULAR((3,)),
        ],
        compiler_params=pltpu.CompilerParams(
            collective_id=0, has_side_effects=True, vmem_limit_bytes=56 * 1024 * 1024
        ),
    )(acts, cotangent, down_weight.T, project, queries)
    return scores.T


def solution(mesh):
    placed = (
        P("dp", "tensor"),
        P(("dp", "tensor"), None),
        P("tensor", None),
        P("tensor", None),
        P("dp", "tensor"),
    )
    return jax.shard_map(
        shards, mesh=mesh, in_specs=placed, out_specs=P("dp", None), check_vma=False
    )
```

```python
import functools

import jax
import jax.numpy as jnp
from jax import lax
from jax.experimental import pallas as pl
from jax.experimental.pallas import tpu as pltpu
from jax.sharding import PartitionSpec as P

RANK = 16
PK = 512
SEQS = 64
MESH = pl.DeviceIdType.MESH
F32 = jnp.float32
BF16 = jnp.bfloat16

PARTNERS = ((1, 2), (0, 2), (1, 1), (1, 3), (0, 1), (1, 0), (0, 3))
AWAY = (14, 13, 15, 12, 4, 11, 8, 3, 5, 10, 9, 2, 6, 1, 7)
NEAR = 13
DOUBLINGS = 7


def doubling_constants():
    t, c = 130.0 / 128.0, []
    for _ in range(DOUBLINGS):
        c.append(2 * t * t / (2 * t * t - 1))
        t = 2 * t * t - 1
    return c


def nt(a, b):
    return lax.dot_general(
        a, b, (((1,), (1,)), ((), ())), preferred_element_type=F32
    )


def start(other, e):
    if e < NEAR:
        return 16 * (other * NEAR + e)
    return 16 * (2 * NEAR + other * (16 - NEAR) + e - NEAR)


def split(a):
    high = a.astype(BF16)
    return high, (a - high.astype(F32)).astype(BF16)


def product(lefts, right):
    rows = []
    for left in lefts:
        high, low = split(left)
        lane = lax.broadcasted_iota(jnp.int32, left.shape, 1)
        rows.append(jnp.where(lane < 64, high, low))
    left = jnp.concatenate(rows, axis=0)
    high, low = split(right)
    return jnp.dot(
        jnp.concatenate([left, left], axis=1),
        jnp.concatenate([high, high, low, low], axis=0),
        preferred_element_type=F32,
    )


def take(sem, like):
    pltpu.make_async_copy(like, like, sem).wait()


def kernel(
    acts, cot, down, proj, queries, out,
    acts_v, cot_v, down_v, proj_v, q_v,
    send1, recv1, send2, recv2, parts, send3, recv3, table, wide,
    send_k, recv_k, send_c, recv_c,
    load_sem, acts_sem, s_sem, r_sem, relay,
):
    dp, me = lax.axis_index("dp"), lax.axis_index("tensor")
    x, y = me // 4, lax.rem(me, 4)
    core, spot = lax.rem(dp, 2), dp // 2
    sibling = dp + 1 - 2 * core

    def partner(dx, dy):
        return lax.rem(x + dx, 2) * 4 + lax.rem(y + dy, 4)

    def along(dx, dz):
        return lax.rem(spot // 8 + dx, 2) * 16 + lax.rem(spot + dz, 8) * 2 + core

    def post(src, dst, stage, device):
        copy = pltpu.make_async_remote_copy(
            src_ref=src, dst_ref=dst, send_sem=s_sem.at[stage], recv_sem=r_sem.at[stage],
            device_id=device, device_id_type=MESH,
        )
        copy.start()

    loads = []

    def load(src, dst, sem):
        copy = pltpu.make_async_copy(src, dst, sem)
        copy.start()
        return copy

    order = [partner(dx, dy) for dx, dy in PARTNERS] + [me]
    down_copy = load(down, down_v, load_sem.at[0])
    acts_copies = []

    def load_acts(i):
        tokens = pl.ds(pl.multiple_of(order[i] * 256, 256), 256)
        acts_copies.append(load(acts.at[tokens], acts_v.at[pl.ds(i * 256, 256)], acts_sem.at[i]))

    for i in range(4):
        load_acts(i)

    barrier = pltpu.get_barrier_semaphore()
    for p in order[:-1]:
        pl.semaphore_signal(barrier, inc=1, device_id={"tensor": p}, device_id_type=MESH)
    pl.semaphore_signal(barrier, inc=1, device_id={"dp": sibling}, device_id_type=MESH)
    close = [along(1, 0)] + [along(0, dz) for dz in (2, 6, 1, 7)]
    for there in close:
        pl.semaphore_signal(barrier, inc=1, device_id={"dp": there}, device_id_type=MESH)

    for i in range(4, 8):
        load_acts(i)

    down_copy.wait()
    down_t = down_v[...]
    for pair in range(4):
        acts_copies[2 * pair].wait()
        acts_copies[2 * pair + 1].wait()
        part = nt(down_t, acts_v[pl.ds(pair * 512, 512), :])
        send1[2 * pair] = part[:, :256]
        if pair < 3:
            send1[2 * pair + 1] = part[:, 256:]
        else:
            recv1[me] = part[:, 256:]
        if pair == 1:
            for i in range(4):
                tokens = pl.ds(i * 64, 64)
                load(cot.at[tokens], cot_v.at[tokens], load_sem.at[1])
            proj_copy = load(proj, proj_v, load_sem.at[2])
            q_copy = load(queries, q_v, load_sem.at[3])
            pl.semaphore_wait(barrier, 13)
            for i in range(2):
                post(send1.at[i], recv1.at[me], 0, {"tensor": order[i]})
        if pair > 0:
            for i in range(2 * pair, min(2 * pair + 2, 7)):
                post(send1.at[i], recv1.at[me], 0, {"tensor": order[i]})
    for dz in (2, 6):
        pl.semaphore_signal(relay.at[0], inc=1, device_id={"dp": along(0, dz)}, device_id_type=MESH)
    take(r_sem.at[0], recv1.at[pl.ds(0, 7)])
    inputs = recv1[0]
    for t in range(1, 8):
        inputs = inputs + recv1[t]
    inputs = inputs.astype(BF16)

    take(load_sem.at[1], cot_v)
    own_rows = pl.ds(pl.multiple_of(me * 16, 16), 16)
    for i, p in enumerate(order):
        features = pl.ds(pl.multiple_of(p * 1024, 1024), 1024)
        grad = jnp.dot(inputs, cot_v[:, features], preferred_element_type=F32).astype(BF16)
        if i < 7:
            send2[i] = grad
            post(send2.at[i], recv2.at[own_rows], 1, {"tensor": p})
        else:
            recv2[own_rows, :] = grad
    pl.semaphore_wait(relay.at[0], 2)
    pl.semaphore_signal(relay.at[1], inc=1, device_id={"dp": along(1, 0)}, device_id_type=MESH)
    pl.semaphore_wait(relay.at[1], 1)
    pl.semaphore_signal(relay.at[2], inc=1, device_id={"dp": sibling}, device_id_type=MESH)
    proj_copy.wait()
    take(r_sem.at[1], recv2.at[pl.ds(0, 112)])

    projected = jnp.dot(recv2[...], proj_v[...], preferred_element_type=F32)
    for s in range(2):
        total = projected[64 * s:64 * s + 16]
        for t in range(1, 4):
            total = total + projected[64 * s + 16 * t:64 * s + 16 * t + 16]
        for q in range(4):
            parts[32 * q + 16 * s:32 * q + 16 * s + 16, :] = total[:, 128 * q:128 * q + 128]
    for s in range(2):
        for i in range(2):
            for q in range(4):
                send3[pl.ds(s * 8 + i * 4 + q, 8, stride=16), :] = parts[
                    pl.ds(32 * q + 16 * s + i, 8, stride=2), :
                ]
    for i, p in enumerate(order[:-1]):
        block = pl.ds(pl.multiple_of(p * 16, 16), 16)
        post(send3.at[block], recv3.at[me], 2, {"tensor": p})
    recv3[me] = send3[pl.ds(pl.multiple_of(me * 16, 16), 16), :]
    take(r_sem.at[2], recv3.at[pl.ds(0, 7)])
    mine = recv3[0]
    for t in range(1, 8):
        mine = mine + recv3[t]

    table[0:16, :] = mine.astype(BF16)
    pl.semaphore_wait(relay.at[2], 1)
    own = table.at[pl.ds(0, 16)]
    near = pl.ds(0, 16 * NEAR)
    for e in AWAY:
        back = 8 - e if e < 8 else 8 + (20 - e) % 8
        there = along(e // 8, (e - 2 * (e // 8)) % 8)
        stage = 3 if e >= NEAR else 4
        post(own, table.at[pl.ds(start(0, back), 16)], stage, {"dp": there})
        post(own, table.at[pl.ds(start(1, back), 16)], stage, {"dp": there + 1 - 2 * core})
    post(own, table.at[pl.ds(start(1, 0), 16)], 4, {"dp": sibling})
    take(r_sem.at[4], table.at[pl.ds(0, 16 * (2 * NEAR - 1))])
    q_copy.wait()
    both_near, far = pl.ds(0, 32 * NEAR), pl.ds(32 * NEAR, 32 * (16 - NEAR))
    wide[both_near, :] = table[both_near, :].astype(F32)
    take(r_sem.at[3], table.at[far])
    wide[far, :] = table[far, :].astype(F32)

    pieces = [wide[pl.ds(j, 64, stride=8), :].astype(BF16) for j in range(8)]
    whole = jnp.concatenate(pieces, axis=1)
    gram = nt(whole, jnp.concatenate([whole, whole], axis=0))
    lane = lax.broadcasted_iota(jnp.int32, (32, 128), 1)
    gram = jnp.where(lane < 64, gram[:32], gram[32:])
    send_k[...] = gram
    for p in order[:-1]:
        post(send_k, recv_k.at[me], 5, {"tensor": p})
    recv_k[me] = gram
    cross = nt(whole, q_v[...]).astype(BF16)
    send_c[...] = cross
    for p in order[:-1]:
        post(send_c, recv_c.at[me], 6, {"tensor": p})
    recv_c[me] = cross

    take(r_sem.at[5], recv_k.at[pl.ds(0, 7)])
    gram = recv_k[0]
    for t in range(1, 8):
        gram = gram + recv_k[t]
    turned = pltpu.roll(gram, 64, 1)
    gram = jnp.concatenate(
        [jnp.where(lane < 64, gram, turned), jnp.where(lane < 64, turned, gram)], axis=0
    )
    row = lax.broadcasted_iota(jnp.int32, (64, 128), 0)
    column = lax.rem(lax.broadcasted_iota(jnp.int32, (64, 128), 1), 64)
    eye = (row == column).astype(F32)
    unit = 256.0 / (65.0 * jnp.sum(gram * eye, keepdims=True))
    w = (1.0 - 1.0 / 65.0) * eye - gram * unit
    block = column // 2
    near_block = block < 2 * NEAR
    other = jnp.where(near_block, block // NEAR, (block - 2 * NEAR) // (16 - NEAR))
    e = jnp.where(
        near_block, lax.rem(block, NEAR), NEAR + lax.rem(block - 2 * NEAR + 16 - NEAR, 16 - NEAR)
    )
    dx = e // 8
    place = lax.rem(spot // 8 + dx, 2) * 32 + lax.rem(lax.rem(spot, 8) + e - 2 * dx + 8, 8) * 4
    place = place + lax.rem(core + other, 2) * 2 + lax.rem(column, 2)
    place = (place == row).astype(F32)
    inverse = place
    scale = 64.0
    constants = doubling_constants()
    for j in range(DOUBLINGS):
        scale = scale * constants[j]
        if j < DOUBLINGS - 1:
            products = product([w, inverse], w)
            inverse = inverse + products[64:]
            w = constants[j] * products[:64] - (constants[j] - 1.0) * eye
        else:
            inverse = inverse + product([inverse], w)
    inverse = inverse * (unit * scale)

    take(s_sem.at[0], send1.at[pl.ds(0, 7)])
    take(s_sem.at[1], send2.at[pl.ds(0, 7)])
    take(s_sem.at[2], send3.at[pl.ds(0, 112)])
    take(s_sem.at[3], table.at[far])
    take(s_sem.at[4], table.at[pl.ds(0, 16 * (2 * NEAR - 1))])

    take(r_sem.at[6], recv_c.at[pl.ds(0, 7)])
    cross = recv_c[0].astype(F32)
    for t in range(1, 8):
        cross = cross + recv_c[t].astype(F32)
    out[...] = product([inverse], cross)
    take(s_sem.at[5], recv_k.at[pl.ds(0, 7)])
    take(s_sem.at[6], recv_c.at[pl.ds(0, 7)])


def shards(acts, cotangent, down_weight, project, queries):
    v = pltpu.VMEM
    scores = pl.pallas_call(
        kernel,
        out_shape=pltpu.VMEM((64, 128), F32),
        in_specs=[pl.BlockSpec(memory_space=pl.ANY)] * 5,
        out_specs=pl.BlockSpec(memory_space=pltpu.VMEM),
        scratch_shapes=[
            v((2048, 1024), BF16), v((256, 8192), BF16), v((16, 1024), BF16),
            v((1024, 512), BF16), v((128, 1024), BF16),
            v((8, 16, 256), F32), v((8, 16, 256), F32),
            v((8, 16, 1024), BF16), v((128, 1024), BF16),
            v((128, 128), F32), v((128, 128), F32), v((8, 16, 128), F32), v((512, 128), BF16), v((512, 128), F32),
            v((32, 128), F32), v((8, 32, 128), F32), v((64, 128), BF16), v((8, 64, 128), BF16),
            pltpu.SemaphoreType.DMA((4,)), pltpu.SemaphoreType.DMA((8,)),
            pltpu.SemaphoreType.DMA((8,)), pltpu.SemaphoreType.DMA((8,)),
            pltpu.SemaphoreType.REGULAR((3,)),
        ],
        compiler_params=pltpu.CompilerParams(
            collective_id=0, has_side_effects=True, vmem_limit_bytes=56 * 1024 * 1024
        ),
    )(acts, cotangent, down_weight.T, project, queries)
    return scores.T


def solution(mesh):
    placed = (
        P("dp", "tensor"),
        P(("dp", "tensor"), None),
        P("tensor", None),
        P("tensor", None),
        P("dp", "tensor"),
    )
    return jax.shard_map(
        shards, mesh=mesh, in_specs=placed, out_specs=P("dp", None), check_vma=False
    )
```

```python
import functools

import jax
import jax.numpy as jnp
from jax import lax
from jax.experimental import pallas as pl
from jax.experimental.pallas import tpu as pltpu
from jax.sharding import PartitionSpec as P

RANK = 16
PK = 512
SEQS = 64
MESH = pl.DeviceIdType.MESH
F32 = jnp.float32
BF16 = jnp.bfloat16

PARTNERS = ((0, 2), (1, 2), (0, 1), (1, 1), (1, 3), (0, 3), (1, 0))
AWAY = (14, 13, 15, 12, 4, 11, 8, 3, 5, 10, 9, 2, 6, 1, 7)
NEAR = 13
DOUBLINGS = 7


def doubling_constants():
    t, c = 130.0 / 128.0, []
    for _ in range(DOUBLINGS):
        c.append(2 * t * t / (2 * t * t - 1))
        t = 2 * t * t - 1
    return c


def nt(a, b):
    return lax.dot_general(
        a, b, (((1,), (1,)), ((), ())), preferred_element_type=F32
    )


def start(other, e):
    if e < NEAR:
        return 16 * (other * NEAR + e)
    return 16 * (2 * NEAR + other * (16 - NEAR) + e - NEAR)


def split(a):
    high = a.astype(BF16)
    return high, (a - high.astype(F32)).astype(BF16)


def product(lefts, right):
    rows = []
    for left in lefts:
        high, low = split(left)
        lane = lax.broadcasted_iota(jnp.int32, left.shape, 1)
        rows.append(jnp.where(lane < 64, high, low))
    left = jnp.concatenate(rows, axis=0)
    high, low = split(right)
    return jnp.dot(
        jnp.concatenate([left, left], axis=1),
        jnp.concatenate([high, high, low, low], axis=0),
        preferred_element_type=F32,
    )


def take(sem, like):
    pltpu.make_async_copy(like, like, sem).wait()


def kernel(
    acts, cot, down, proj, queries, out,
    acts_v, cot_v, down_v, proj_v, q_v,
    send1, recv1, send2, recv2, parts, send3, recv3, table, wide,
    send_k, recv_k, send_c, recv_c,
    load_sem, acts_sem, s_sem, r_sem, relay,
):
    dp, me = lax.axis_index("dp"), lax.axis_index("tensor")
    x, y = me // 4, lax.rem(me, 4)
    core, spot = lax.rem(dp, 2), dp // 2
    sibling = dp + 1 - 2 * core

    def partner(dx, dy):
        return lax.rem(x + dx, 2) * 4 + lax.rem(y + dy, 4)

    def along(dx, dz):
        return lax.rem(spot // 8 + dx, 2) * 16 + lax.rem(spot + dz, 8) * 2 + core

    def post(src, dst, stage, device):
        copy = pltpu.make_async_remote_copy(
            src_ref=src, dst_ref=dst, send_sem=s_sem.at[stage], recv_sem=r_sem.at[stage],
            device_id=device, device_id_type=MESH,
        )
        copy.start()

    loads = []

    def load(src, dst, sem):
        copy = pltpu.make_async_copy(src, dst, sem)
        copy.start()
        return copy

    order = [partner(dx, dy) for dx, dy in PARTNERS] + [me]
    down_copy = load(down, down_v, load_sem.at[0])
    acts_copies = []

    def load_acts(i):
        tokens = pl.ds(pl.multiple_of(order[i] * 256, 256), 256)
        acts_copies.append(load(acts.at[tokens], acts_v.at[pl.ds(i * 256, 256)], acts_sem.at[i]))

    for i in range(4):
        load_acts(i)

    barrier = pltpu.get_barrier_semaphore()
    for p in order[:-1]:
        pl.semaphore_signal(barrier, inc=1, device_id={"tensor": p}, device_id_type=MESH)
    pl.semaphore_signal(barrier, inc=1, device_id={"dp": sibling}, device_id_type=MESH)
    close = [along(1, 0)] + [along(0, dz) for dz in (2, 6, 1, 7)]
    for there in close:
        pl.semaphore_signal(barrier, inc=1, device_id={"dp": there}, device_id_type=MESH)

    for i in range(4, 8):
        load_acts(i)

    down_copy.wait()
    down_t = down_v[...]
    for pair in range(4):
        acts_copies[2 * pair].wait()
        acts_copies[2 * pair + 1].wait()
        part = nt(down_t, acts_v[pl.ds(pair * 512, 512), :])
        send1[2 * pair] = part[:, :256]
        if pair < 3:
            send1[2 * pair + 1] = part[:, 256:]
        else:
            recv1[me] = part[:, 256:]
        if pair == 1:
            for i in range(4):
                tokens = pl.ds(i * 64, 64)
                load(cot.at[tokens], cot_v.at[tokens], load_sem.at[1])
            proj_copy = load(proj, proj_v, load_sem.at[2])
            q_copy = load(queries, q_v, load_sem.at[3])
            pl.semaphore_wait(barrier, 13)
            for i in range(2):
                post(send1.at[i], recv1.at[me], 0, {"tensor": order[i]})
        if pair > 0:
            for i in range(2 * pair, min(2 * pair + 2, 7)):
                post(send1.at[i], recv1.at[me], 0, {"tensor": order[i]})
    for dz in (2, 6):
        pl.semaphore_signal(relay.at[0], inc=1, device_id={"dp": along(0, dz)}, device_id_type=MESH)
    take(r_sem.at[0], recv1.at[pl.ds(0, 7)])
    inputs = recv1[0]
    for t in range(1, 8):
        inputs = inputs + recv1[t]
    inputs = inputs.astype(BF16)

    take(load_sem.at[1], cot_v)
    own_rows = pl.ds(pl.multiple_of(me * 16, 16), 16)
    for i, p in enumerate(order):
        features = pl.ds(pl.multiple_of(p * 1024, 1024), 1024)
        grad = jnp.dot(inputs, cot_v[:, features], preferred_element_type=F32).astype(BF16)
        if i < 7:
            send2[i] = grad
            post(send2.at[i], recv2.at[own_rows], 1, {"tensor": p})
        else:
            recv2[own_rows, :] = grad
    pl.semaphore_wait(relay.at[0], 2)
    pl.semaphore_signal(relay.at[1], inc=1, device_id={"dp": along(1, 0)}, device_id_type=MESH)
    pl.semaphore_wait(relay.at[1], 1)
    pl.semaphore_signal(relay.at[2], inc=1, device_id={"dp": sibling}, device_id_type=MESH)
    proj_copy.wait()
    take(r_sem.at[1], recv2.at[pl.ds(0, 112)])

    projected = jnp.dot(recv2[...], proj_v[...], preferred_element_type=F32)
    for s in range(2):
        total = projected[64 * s:64 * s + 16]
        for t in range(1, 4):
            total = total + projected[64 * s + 16 * t:64 * s + 16 * t + 16]
        for q in range(4):
            parts[32 * q + 16 * s:32 * q + 16 * s + 16, :] = total[:, 128 * q:128 * q + 128]
    for s in range(2):
        for i in range(2):
            for q in range(4):
                send3[pl.ds(s * 8 + i * 4 + q, 8, stride=16), :] = parts[
                    pl.ds(32 * q + 16 * s + i, 8, stride=2), :
                ]
    for i, p in enumerate(order[:-1]):
        block = pl.ds(pl.multiple_of(p * 16, 16), 16)
        post(send3.at[block], recv3.at[me], 2, {"tensor": p})
    recv3[me] = send3[pl.ds(pl.multiple_of(me * 16, 16), 16), :]
    take(r_sem.at[2], recv3.at[pl.ds(0, 7)])
    mine = recv3[0]
    for t in range(1, 8):
        mine = mine + recv3[t]

    table[0:16, :] = mine.astype(BF16)
    pl.semaphore_wait(relay.at[2], 1)
    own = table.at[pl.ds(0, 16)]
    near = pl.ds(0, 16 * NEAR)
    for e in AWAY:
        back = 8 - e if e < 8 else 8 + (20 - e) % 8
        there = along(e // 8, (e - 2 * (e // 8)) % 8)
        stage = 3 if e >= NEAR else 4
        post(own, table.at[pl.ds(start(1, back), 16)], stage, {"dp": there + 1 - 2 * core})
        post(own, table.at[pl.ds(start(0, back), 16)], stage, {"dp": there})
    post(own, table.at[pl.ds(start(1, 0), 16)], 4, {"dp": sibling})
    take(r_sem.at[4], table.at[pl.ds(0, 16 * (2 * NEAR - 1))])
    q_copy.wait()
    both_near, far = pl.ds(0, 32 * NEAR), pl.ds(32 * NEAR, 32 * (16 - NEAR))
    wide[both_near, :] = table[both_near, :].astype(F32)
    take(r_sem.at[3], table.at[far])
    wide[far, :] = table[far, :].astype(F32)

    pieces = [wide[pl.ds(j, 64, stride=8), :].astype(BF16) for j in range(8)]
    whole = jnp.concatenate(pieces, axis=1)
    gram = nt(whole, jnp.concatenate([whole, whole], axis=0))
    lane = lax.broadcasted_iota(jnp.int32, (32, 128), 1)
    gram = jnp.where(lane < 64, gram[:32], gram[32:])
    send_k[...] = gram
    for p in order[:-1]:
        post(send_k, recv_k.at[me], 5, {"tensor": p})
    recv_k[me] = gram
    cross = nt(whole, q_v[...]).astype(BF16)
    send_c[...] = cross
    for p in order[:-1]:
        post(send_c, recv_c.at[me], 6, {"tensor": p})
    recv_c[me] = cross

    take(r_sem.at[5], recv_k.at[pl.ds(0, 7)])
    gram = recv_k[0]
    for t in range(1, 8):
        gram = gram + recv_k[t]
    turned = pltpu.roll(gram, 64, 1)
    gram = jnp.concatenate(
        [jnp.where(lane < 64, gram, turned), jnp.where(lane < 64, turned, gram)], axis=0
    )
    row = lax.broadcasted_iota(jnp.int32, (64, 128), 0)
    column = lax.rem(lax.broadcasted_iota(jnp.int32, (64, 128), 1), 64)
    eye = (row == column).astype(F32)
    unit = 256.0 / (65.0 * jnp.sum(gram * eye, keepdims=True))
    w = (1.0 - 1.0 / 65.0) * eye - gram * unit
    block = column // 2
    near_block = block < 2 * NEAR
    other = jnp.where(near_block, block // NEAR, (block - 2 * NEAR) // (16 - NEAR))
    e = jnp.where(
        near_block, lax.rem(block, NEAR), NEAR + lax.rem(block - 2 * NEAR + 16 - NEAR, 16 - NEAR)
    )
    dx = e // 8
    place = lax.rem(spot // 8 + dx, 2) * 32 + lax.rem(lax.rem(spot, 8) + e - 2 * dx + 8, 8) * 4
    place = place + lax.rem(core + other, 2) * 2 + lax.rem(column, 2)
    place = (place == row).astype(F32)
    inverse = place
    scale = 64.0
    constants = doubling_constants()
    for j in range(DOUBLINGS):
        scale = scale * constants[j]
        if j < DOUBLINGS - 1:
            products = product([w, inverse], w)
            inverse = inverse + products[64:]
            w = constants[j] * products[:64] - (constants[j] - 1.0) * eye
        else:
            inverse = inverse + product([inverse], w)
    inverse = inverse * (unit * scale)

    take(s_sem.at[0], send1.at[pl.ds(0, 7)])
    take(s_sem.at[1], send2.at[pl.ds(0, 7)])
    take(s_sem.at[2], send3.at[pl.ds(0, 112)])
    take(s_sem.at[3], table.at[far])
    take(s_sem.at[4], table.at[pl.ds(0, 16 * (2 * NEAR - 1))])

    take(r_sem.at[6], recv_c.at[pl.ds(0, 7)])
    cross = recv_c[0].astype(F32)
    for t in range(1, 8):
        cross = cross + recv_c[t].astype(F32)
    out[...] = product([inverse], cross)
    take(s_sem.at[5], recv_k.at[pl.ds(0, 7)])
    take(s_sem.at[6], recv_c.at[pl.ds(0, 7)])


def shards(acts, cotangent, down_weight, project, queries):
    v = pltpu.VMEM
    scores = pl.pallas_call(
        kernel,
        out_shape=pltpu.VMEM((64, 128), F32),
        in_specs=[pl.BlockSpec(memory_space=pl.ANY)] * 5,
        out_specs=pl.BlockSpec(memory_space=pltpu.VMEM),
        scratch_shapes=[
            v((2048, 1024), BF16), v((256, 8192), BF16), v((16, 1024), BF16),
            v((1024, 512), BF16), v((128, 1024), BF16),
            v((8, 16, 256), F32), v((8, 16, 256), F32),
            v((8, 16, 1024), BF16), v((128, 1024), BF16),
            v((128, 128), F32), v((128, 128), F32), v((8, 16, 128), F32), v((512, 128), BF16), v((512, 128), F32),
            v((32, 128), F32), v((8, 32, 128), F32), v((64, 128), BF16), v((8, 64, 128), BF16),
            pltpu.SemaphoreType.DMA((4,)), pltpu.SemaphoreType.DMA((8,)),
            pltpu.SemaphoreType.DMA((8,)), pltpu.SemaphoreType.DMA((8,)),
            pltpu.SemaphoreType.REGULAR((3,)),
        ],
        compiler_params=pltpu.CompilerParams(
            collective_id=0, has_side_effects=True, vmem_limit_bytes=56 * 1024 * 1024
        ),
    )(acts, cotangent, down_weight.T, project, queries)
    return scores.T


def solution(mesh):
    placed = (
        P("dp", "tensor"),
        P(("dp", "tensor"), None),
        P("tensor", None),
        P("tensor", None),
        P("dp", "tensor"),
    )
    return jax.shard_map(
        shards, mesh=mesh, in_specs=placed, out_specs=P("dp", None), check_vma=False
    )
```

```python
import functools

import jax
import jax.numpy as jnp
from jax import lax
from jax.experimental import pallas as pl
from jax.experimental.pallas import tpu as pltpu
from jax.sharding import PartitionSpec as P

RANK = 16
PK = 512
SEQS = 64
MESH = pl.DeviceIdType.MESH
F32 = jnp.float32
BF16 = jnp.bfloat16

PARTNERS = ((0, 2), (1, 2), (0, 1), (1, 1), (1, 3), (0, 3), (1, 0))
AWAY = (14, 13, 15, 12, 4, 11, 8, 3, 5, 10, 9, 2, 6, 1, 7)
NEAR = 13
DOUBLINGS = 7


def doubling_constants():
    t, c = 130.0 / 128.0, []
    for _ in range(DOUBLINGS):
        c.append(2 * t * t / (2 * t * t - 1))
        t = 2 * t * t - 1
    return c


def nt(a, b):
    return lax.dot_general(
        a, b, (((1,), (1,)), ((), ())), preferred_element_type=F32
    )


def start(other, e):
    if e < NEAR:
        return 16 * (other * NEAR + e)
    return 16 * (2 * NEAR + other * (16 - NEAR) + e - NEAR)


def split(a):
    high = a.astype(BF16)
    return high, (a - high.astype(F32)).astype(BF16)


def product(lefts, right):
    rows = []
    for left in lefts:
        high, low = split(left)
        lane = lax.broadcasted_iota(jnp.int32, left.shape, 1)
        rows.append(jnp.where(lane < 64, high, low))
    left = jnp.concatenate(rows, axis=0)
    high, low = split(right)
    return jnp.dot(
        jnp.concatenate([left, left], axis=1),
        jnp.concatenate([high, high, low, low], axis=0),
        preferred_element_type=F32,
    )


def take(sem, like):
    pltpu.make_async_copy(like, like, sem).wait()


def kernel(
    acts, cot, down, proj, queries, out,
    acts_v, cot_v, down_v, proj_v, q_v,
    send1, recv1, send2, recv2, parts, send3, recv3, table, wide,
    send_k, recv_k, send_c, recv_c,
    load_sem, acts_sem, s_sem, r_sem, relay,
):
    dp, me = lax.axis_index("dp"), lax.axis_index("tensor")
    x, y = me // 4, lax.rem(me, 4)
    core, spot = lax.rem(dp, 2), dp // 2
    sibling = dp + 1 - 2 * core

    def partner(dx, dy):
        return lax.rem(x + dx, 2) * 4 + lax.rem(y + dy, 4)

    def along(dx, dz):
        return lax.rem(spot // 8 + dx, 2) * 16 + lax.rem(spot + dz, 8) * 2 + core

    def post(src, dst, stage, device):
        copy = pltpu.make_async_remote_copy(
            src_ref=src, dst_ref=dst, send_sem=s_sem.at[stage], recv_sem=r_sem.at[stage],
            device_id=device, device_id_type=MESH,
        )
        copy.start()

    loads = []

    def load(src, dst, sem):
        copy = pltpu.make_async_copy(src, dst, sem)
        copy.start()
        return copy

    order = [partner(dx, dy) for dx, dy in PARTNERS] + [me]
    down_copy = load(down, down_v, load_sem.at[0])
    acts_copies = []

    def load_acts(i):
        tokens = pl.ds(pl.multiple_of(order[i] * 256, 256), 256)
        acts_copies.append(load(acts.at[tokens], acts_v.at[pl.ds(i * 256, 256)], acts_sem.at[i]))

    for i in range(4):
        load_acts(i)

    barrier = pltpu.get_barrier_semaphore()
    for p in order[:-1]:
        pl.semaphore_signal(barrier, inc=1, device_id={"tensor": p}, device_id_type=MESH)
    pl.semaphore_signal(barrier, inc=1, device_id={"dp": sibling}, device_id_type=MESH)
    close = [along(1, 0)] + [along(0, dz) for dz in (2, 6, 1, 7)]
    for there in close:
        pl.semaphore_signal(barrier, inc=1, device_id={"dp": there}, device_id_type=MESH)

    for i in range(4, 8):
        load_acts(i)

    down_copy.wait()
    down_t = down_v[...]
    for pair in range(4):
        acts_copies[2 * pair].wait()
        acts_copies[2 * pair + 1].wait()
        part = nt(down_t, acts_v[pl.ds(pair * 512, 512), :])
        send1[2 * pair] = part[:, :256]
        if pair < 3:
            send1[2 * pair + 1] = part[:, 256:]
        else:
            recv1[me] = part[:, 256:]
        if pair == 1:
            for i in range(4):
                tokens = pl.ds(i * 64, 64)
                load(cot.at[tokens], cot_v.at[tokens], load_sem.at[1])
            proj_copy = load(proj, proj_v, load_sem.at[2])
            q_copy = load(queries, q_v, load_sem.at[3])
            pl.semaphore_wait(barrier, 13)
            for i in range(2):
                post(send1.at[i], recv1.at[me], 0, {"tensor": order[i]})
        if pair > 0:
            for i in range(2 * pair, min(2 * pair + 2, 7)):
                post(send1.at[i], recv1.at[me], 0, {"tensor": order[i]})
    for dz in (2, 6):
        pl.semaphore_signal(relay.at[0], inc=1, device_id={"dp": along(0, dz)}, device_id_type=MESH)
    take(r_sem.at[0], recv1.at[pl.ds(0, 7)])
    inputs = recv1[0]
    for t in range(1, 8):
        inputs = inputs + recv1[t]
    inputs = inputs.astype(BF16)

    take(load_sem.at[1], cot_v)
    own_rows = pl.ds(pl.multiple_of(me * 16, 16), 16)
    for i, p in enumerate(order):
        features = pl.ds(pl.multiple_of(p * 1024, 1024), 1024)
        grad = jnp.dot(inputs, cot_v[:, features], preferred_element_type=F32).astype(BF16)
        if i < 7:
            send2[i] = grad
            post(send2.at[i], recv2.at[own_rows], 1, {"tensor": p})
        else:
            recv2[own_rows, :] = grad
    pl.semaphore_wait(relay.at[0], 2)
    pl.semaphore_signal(relay.at[1], inc=1, device_id={"dp": along(1, 0)}, device_id_type=MESH)
    pl.semaphore_wait(relay.at[1], 1)
    pl.semaphore_signal(relay.at[2], inc=1, device_id={"dp": sibling}, device_id_type=MESH)
    proj_copy.wait()
    take(r_sem.at[1], recv2.at[pl.ds(0, 112)])

    projected = jnp.dot(recv2[...], proj_v[...], preferred_element_type=F32)
    for s in range(2):
        total = projected[64 * s:64 * s + 16]
        for t in range(1, 4):
            total = total + projected[64 * s + 16 * t:64 * s + 16 * t + 16]
        for q in range(4):
            parts[32 * q + 16 * s:32 * q + 16 * s + 16, :] = total[:, 128 * q:128 * q + 128]
    for s in range(2):
        for i in range(2):
            for q in range(4):
                send3[pl.ds(s * 8 + i * 4 + q, 8, stride=16), :] = parts[
                    pl.ds(32 * q + 16 * s + i, 8, stride=2), :
                ]
    for i, p in enumerate(order[:-1]):
        block = pl.ds(pl.multiple_of(p * 16, 16), 16)
        post(send3.at[block], recv3.at[me], 2, {"tensor": p})
    recv3[me] = send3[pl.ds(pl.multiple_of(me * 16, 16), 16), :]
    take(r_sem.at[2], recv3.at[pl.ds(0, 7)])
    mine = recv3[0]
    for t in range(1, 8):
        mine = mine + recv3[t]

    table[0:16, :] = mine.astype(BF16)
    pl.semaphore_wait(relay.at[2], 1)
    own = table.at[pl.ds(0, 16)]
    near = pl.ds(0, 16 * NEAR)
    for e in AWAY:
        back = 8 - e if e < 8 else 8 + (20 - e) % 8
        there = along(e // 8, (e - 2 * (e // 8)) % 8)
        stage = 3 if e >= NEAR else 4
        post(own, table.at[pl.ds(start(1, back), 16)], stage, {"dp": there + 1 - 2 * core})
        post(own, table.at[pl.ds(start(0, back), 16)], stage, {"dp": there})
    post(own, table.at[pl.ds(start(1, 0), 16)], 4, {"dp": sibling})
    take(r_sem.at[4], table.at[pl.ds(0, 16 * (2 * NEAR - 1))])
    q_copy.wait()
    both_near, far = pl.ds(0, 32 * NEAR), pl.ds(32 * NEAR, 32 * (16 - NEAR))
    wide[both_near, :] = table[both_near, :].astype(F32)

    pieces = [wide[pl.ds(j, 48, stride=8), :].astype(BF16) for j in range(8)]
    first = jnp.concatenate(pieces, axis=1)
    first_cross = nt(first, q_v[...]).astype(BF16)
    take(r_sem.at[3], table.at[far])
    wide[far, :] = table[far, :].astype(F32)
    pieces = [wide[pl.ds(384 + j, 16, stride=8), :].astype(BF16) for j in range(8)]
    rest = jnp.concatenate(pieces, axis=1)
    whole = jnp.concatenate([first, rest], axis=0)
    gram = nt(whole, jnp.concatenate([whole, whole], axis=0))
    lane = lax.broadcasted_iota(jnp.int32, (32, 128), 1)
    gram = jnp.where(lane < 64, gram[:32], gram[32:])
    send_k[...] = gram
    for p in order[:-1]:
        post(send_k, recv_k.at[me], 5, {"tensor": p})
    recv_k[me] = gram
    cross = jnp.concatenate([first_cross, nt(rest, q_v[...]).astype(BF16)], axis=0)
    send_c[...] = cross
    for p in order[:-1]:
        post(send_c, recv_c.at[me], 6, {"tensor": p})
    recv_c[me] = cross

    take(r_sem.at[5], recv_k.at[pl.ds(0, 7)])
    gram = recv_k[0]
    for t in range(1, 8):
        gram = gram + recv_k[t]
    turned = pltpu.roll(gram, 64, 1)
    gram = jnp.concatenate(
        [jnp.where(lane < 64, gram, turned), jnp.where(lane < 64, turned, gram)], axis=0
    )
    row = lax.broadcasted_iota(jnp.int32, (64, 128), 0)
    column = lax.rem(lax.broadcasted_iota(jnp.int32, (64, 128), 1), 64)
    eye = (row == column).astype(F32)
    unit = 256.0 / (65.0 * jnp.sum(gram * eye, keepdims=True))
    w = (1.0 - 1.0 / 65.0) * eye - gram * unit
    block = column // 2
    near_block = block < 2 * NEAR
    other = jnp.where(near_block, block // NEAR, (block - 2 * NEAR) // (16 - NEAR))
    e = jnp.where(
        near_block, lax.rem(block, NEAR), NEAR + lax.rem(block - 2 * NEAR + 16 - NEAR, 16 - NEAR)
    )
    dx = e // 8
    place = lax.rem(spot // 8 + dx, 2) * 32 + lax.rem(lax.rem(spot, 8) + e - 2 * dx + 8, 8) * 4
    place = place + lax.rem(core + other, 2) * 2 + lax.rem(column, 2)
    place = (place == row).astype(F32)
    inverse = place
    scale = 64.0
    constants = doubling_constants()
    for j in range(DOUBLINGS):
        scale = scale * constants[j]
        if j < DOUBLINGS - 1:
            products = product([w, inverse], w)
            inverse = inverse + products[64:]
            w = constants[j] * products[:64] - (constants[j] - 1.0) * eye
        else:
            inverse = inverse + product([inverse], w)
    inverse = inverse * (unit * scale)

    take(s_sem.at[0], send1.at[pl.ds(0, 7)])
    take(s_sem.at[1], send2.at[pl.ds(0, 7)])
    take(s_sem.at[2], send3.at[pl.ds(0, 112)])
    take(s_sem.at[3], table.at[far])
    take(s_sem.at[4], table.at[pl.ds(0, 16 * (2 * NEAR - 1))])

    take(r_sem.at[6], recv_c.at[pl.ds(0, 7)])
    cross = recv_c[0].astype(F32)
    for t in range(1, 8):
        cross = cross + recv_c[t].astype(F32)
    out[...] = product([inverse], cross)
    take(s_sem.at[5], recv_k.at[pl.ds(0, 7)])
    take(s_sem.at[6], recv_c.at[pl.ds(0, 7)])


def shards(acts, cotangent, down_weight, project, queries):
    v = pltpu.VMEM
    scores = pl.pallas_call(
        kernel,
        out_shape=pltpu.VMEM((64, 128), F32),
        in_specs=[pl.BlockSpec(memory_space=pl.ANY)] * 5,
        out_specs=pl.BlockSpec(memory_space=pltpu.VMEM),
        scratch_shapes=[
            v((2048, 1024), BF16), v((256, 8192), BF16), v((16, 1024), BF16),
            v((1024, 512), BF16), v((128, 1024), BF16),
            v((8, 16, 256), F32), v((8, 16, 256), F32),
            v((8, 16, 1024), BF16), v((128, 1024), BF16),
            v((128, 128), F32), v((128, 128), F32), v((8, 16, 128), F32), v((512, 128), BF16), v((512, 128), F32),
            v((32, 128), F32), v((8, 32, 128), F32), v((64, 128), BF16), v((8, 64, 128), BF16),
            pltpu.SemaphoreType.DMA((4,)), pltpu.SemaphoreType.DMA((8,)),
            pltpu.SemaphoreType.DMA((8,)), pltpu.SemaphoreType.DMA((8,)),
            pltpu.SemaphoreType.REGULAR((3,)),
        ],
        compiler_params=pltpu.CompilerParams(
            collective_id=0, has_side_effects=True, vmem_limit_bytes=56 * 1024 * 1024
        ),
    )(acts, cotangent, down_weight.T, project, queries)
    return scores.T


def solution(mesh):
    placed = (
        P("dp", "tensor"),
        P(("dp", "tensor"), None),
        P("tensor", None),
        P("tensor", None),
        P("dp", "tensor"),
    )
    return jax.shard_map(
        shards, mesh=mesh, in_specs=placed, out_specs=P("dp", None), check_vma=False
    )
```
